32 devices in a mesh: row: 4 (over y, x), col: 8 (over z, core).
Axes of the slice: x: 2, y: 2, z: 4, core: 2. Of those that a mesh axis runs over, the one named last changes fastest.
Arguments:
- points: float32 [4096, 128], P(('row', 'col')), may hold values from -4 to 4
- labels: int32 [4096], P(('row', 'col')), may hold values from 0 to 63
- coefficients: float32 [4096, 64], P(('row', 'col')), as said below
Outputs:
- new_coefficients: float32 [4096, 64], P(('row', 'col'))
- probabilities: float32 [4096, 64], P(('row', 'col'))
The draws below stay inside these ranges and needn't reach their ends.
Inputs may be any that keep to these rules, and one draw needn't show every extreme that they name: `coefficients`: entries have magnitude at most 300 * sqrt(4096) / 16.
All inputs are finite; a program needn't handle non-finite values.
Results may differ from the reference program's by a relative error of at most 0.012.
The reference program's roundings to bfloat16 on the way count: a program that leaves them out, or rounds other values in their place, can miss the bound.
Values may be sent and summed in bfloat16 or wider, within the bound.
A program may use at most 64 MiB of HBM per device.

```python
import math
import jax
import jax.numpy as jnp
from jax import lax

FEAT = 128
CLASSES = 64
STEPS = 1
NPTS = 4096


def draw_points(key, part):
    key_basis, key_latent, key_noise = jax.random.split(jax.random.fold_in(key, 11), 3)
    sign_table = jnp.where(jax.random.bernoulli(key_basis, 0.5, (16, FEAT)), 1.0, -1.0).astype(jnp.float32) / math.sqrt(FEAT)
    spread = math.sqrt(FEAT / 8.0)
    latent = jax.random.normal(key_latent, (NPTS, 16), jnp.float32)
    noise_part = jax.random.normal(key_noise, (NPTS, FEAT), jnp.float32)
    values = spread * jnp.dot(latent, sign_table, precision=lax.Precision.HIGHEST) + 0.5 * noise_part
    return jnp.clip(values, -4.0, 4.0)


def draw_coefficients(key, part):
    values = jax.random.normal(key, (NPTS, CLASSES), jnp.float32)
    return values


def place_ends(values, stream_key, smallest, high):
    dims = values.shape
    spot = [jax.random.randint(jax.random.fold_in(stream_key, axis), (), 0, dims[axis]) for axis in range(len(dims))]
    values = values.at[tuple(spot)].set(smallest)
    longest = dims.index(max(dims))
    spot[longest] = (spot[longest] + 1) % dims[longest]
    return values.at[tuple(spot)].set(high)


def setup_inputs(seed: int = 0) -> dict:
    keys = jax.random.split(jax.random.key(seed), 4)
    return {
        "points": draw_points(jax.random.fold_in(keys[3], 71), 0),
        "labels": place_ends(jax.random.randint(keys[1], (NPTS,), 0, CLASSES), jax.random.fold_in(keys[1], 1), 0, CLASSES - 1).astype(jnp.int32),
        "coefficients": draw_coefficients(jax.random.fold_in(keys[3], 71), 0),
    }


def kernel_apply(points, current):
    squares = lax.optimization_barrier(jnp.sum(points * points, axis=1))
    block_size = math.gcd(NPTS, 2048)
    blocks = points.reshape(NPTS // block_size, block_size, FEAT)
    block_squares = squares.reshape(NPTS // block_size, block_size)
    rounded = current.astype(jnp.bfloat16)

    def one_block(pair):
        block_points, block_sq = pair
        products = lax.dot_general(block_points, points, (((1,), (1,)), ((), ())), precision=lax.Precision.HIGHEST, preferred_element_type=jnp.float32)
        distance = block_sq[:, None] + squares[None, :] - 2.0 * products
        kernel_rows = jnp.exp(-distance / FEAT).astype(jnp.bfloat16)
        return jnp.dot(kernel_rows, rounded, preferred_element_type=jnp.float32)
    result = lax.map(one_block, (blocks, block_squares))
    return result.reshape(NPTS, CLASSES)

def reference(points, labels, coefficients):
    logit_scale = 16.0 / math.sqrt(NPTS)
    onehot = (labels[:, None] == jnp.arange(CLASSES, dtype=jnp.int32)[None, :]).astype(jnp.float32)
    current = coefficients
    probabilities = jnp.zeros_like(coefficients)
    for iteration in range(STEPS):
        logits = logit_scale * kernel_apply(points, current)
        probabilities = jax.nn.softmax(logits, axis=1)
        residual = logit_scale * (probabilities - onehot)
        current = current - kernel_apply(points, residual)
    return (current, probabilities)
```

```python
import functools
import math

import jax
import jax.numpy as jnp
from jax import lax
from jax.experimental import pallas as pl
from jax.experimental.pallas import tpu as pltpu
from jax.sharding import PartitionSpec as P

MESH = pl.DeviceIdType.MESH
NT = (((1,), (1,)), ((), ()))
NN = (((1,), (0,)), ((), ()))
GATHER_PLANE = False


def split_bf16(x):
    hi = x.astype(jnp.bfloat16)
    lo = (x - hi.astype(jnp.float32)).astype(jnp.bfloat16)
    return hi, lo


def kernel(
    lines, planes, cores, logit_scale,
    points_ref, labels_ref, coef_ref,
    new_ref, prob_ref,
    line_pts, plane_pts, values, tile, partial, landed,
    line_send, line_recv, plane_send, plane_recv, value_send, value_recv, part_send, part_recv,
):
    own, feat = points_ref.shape
    classes = coef_ref.shape[0]
    row = lax.axis_index("row")
    col = lax.axis_index("col")
    my_line = col // cores
    my_plane = row * cores + col % cores

    def line_device(i):
        return (row, i * cores + col % cores)

    def plane_device(j):
        return (j // cores, my_line * cores + j % cores)

    if GATHER_PLANE:
        gathers, my_gather, gather_device, gather_pts = planes, my_plane, plane_device, plane_pts
        reduces, my_reduce, reduce_device, reduce_pts = lines, my_line, line_device, line_pts
    else:
        gathers, my_gather, gather_device, gather_pts = lines, my_line, line_device, line_pts
        reduces, my_reduce, reduce_device, reduce_pts = planes, my_plane, plane_device, plane_pts

    barrier = pltpu.get_barrier_semaphore()
    for k in range(1, lines):
        pl.semaphore_signal(
            barrier, inc=1, device_id=line_device(lax.rem(my_line + k, lines)), device_id_type=MESH
        )
    for k in range(1, planes):
        pl.semaphore_signal(
            barrier, inc=1, device_id=plane_device(lax.rem(my_plane + k, planes)), device_id_type=MESH
        )

    hi, lo = split_bf16(points_ref[...])
    line_pts[my_line, :, :feat] = hi
    line_pts[my_line, :, feat:] = lo
    plane_pts[my_plane, :, :feat] = hi
    plane_pts[my_plane, :, feat:] = lo
    values[0, my_gather] = coef_ref[...].astype(jnp.bfloat16)
    pl.semaphore_wait(barrier, lines + planes - 2)

    def push(src, dst, send, recv, device):
        copy = pltpu.make_async_remote_copy(
            src_ref=src, dst_ref=dst, send_sem=send, recv_sem=recv, device_id=device, device_id_type=MESH
        )
        copy.start()
        return copy

    def recv_wait(buf, sem):
        pltpu.make_async_copy(buf, buf, sem).wait()

    sent = []
    for k in range(1, lines):
        to = lax.rem(my_line + k, lines)
        sent.append(push(line_pts.at[my_line], line_pts.at[my_line], line_send.at[k], line_recv.at[my_line], line_device(to)))
    for k in range(1, planes):
        to = lax.rem(my_plane + k, planes)
        sent.append(push(plane_pts.at[my_plane], plane_pts.at[my_plane], plane_send.at[k], plane_recv.at[my_plane], plane_device(to)))

    def send_values(phase):
        for k in range(1, gathers):
            to = lax.rem(my_gather + k, gathers)
            sent.append(push(
                values.at[phase, my_gather], values.at[phase, my_gather],
                value_send.at[phase, k], value_recv.at[phase, my_gather], gather_device(to),
            ))

    send_values(0)

    def wait_block(group, buf, recv, me, count, k):
        at = lax.rem(me + count - k, count)
        recv_wait(buf.at[at], recv.at[at])
        return at

    reduce_recv = line_recv if GATHER_PLANE else plane_recv
    gather_recv = plane_recv if GATHER_PLANE else line_recv
    for k in range(1, reduces):
        wait_block("reduce", reduce_pts, reduce_recv, my_reduce, reduces, k)
    right = reduce_pts[...].reshape(reduces * own, 2 * feat)
    right_f32 = right[:, :feat].astype(jnp.float32) + right[:, feat:].astype(jnp.float32)
    sq_hi, sq_rest = split_bf16(right_f32 * right_f32)
    right_squares = lax.dot_general(
        jnp.ones((8, 2 * feat), jnp.bfloat16), jnp.concatenate([sq_hi, sq_rest], axis=1), NT,
        preferred_element_type=jnp.float32,
    )[:1]

    for k in range(gathers):
        if k == 0:
            at = my_gather
        else:
            at = wait_block("gather", gather_pts, gather_recv, my_gather, gathers, k)
        left = gather_pts[at]
        left_hi, left_lo = left[:, :feat], left[:, feat:]
        left_f32 = left_hi.astype(jnp.float32) + left_lo.astype(jnp.float32)
        left_squares = jnp.sum(left_f32 * left_f32, axis=1, keepdims=True)
        swapped = jnp.concatenate([left_lo, left_hi], axis=1)
        products = lax.dot_general(left, right, NT, preferred_element_type=jnp.float32)
        products += lax.dot_general(swapped, right, NT, preferred_element_type=jnp.float32)
        distance = left_squares + right_squares - 2.0 * products
        tile[at] = jnp.exp(distance * (-1.0 / feat)).astype(jnp.bfloat16)

    def apply(phase):
        for k in range(1, gathers):
            at = lax.rem(my_gather + gathers - k, gathers)
            recv_wait(values.at[phase, at], value_recv.at[phase, at])
        left = jnp.concatenate([values[phase, i] for i in range(gathers)], axis=1)
        result = lax.dot_general(
            left, tile[...].reshape(gathers * own, reduces * own), NN, preferred_element_type=jnp.float32
        )
        for j in range(reduces):
            partial[phase, j] = result[:, j * own : (j + 1) * own]
        for k in range(1, reduces):
            to = lax.rem(my_reduce + k, reduces)
            sent.append(push(
                partial.at[phase, to], landed.at[phase, my_reduce],
                part_send.at[phase, k], part_recv.at[phase, my_reduce], reduce_device(to),
            ))
        total = partial[phase, my_reduce]
        for k in range(1, reduces):
            at = lax.rem(my_reduce + reduces - k, reduces)
            recv_wait(landed.at[phase, at], part_recv.at[phase, at])
            total += landed[phase, at]
        return total

    logits = logit_scale * apply(0)
    weights = jnp.exp(logits - jnp.max(logits, axis=0, keepdims=True))
    probabilities = weights / jnp.sum(weights, axis=0, keepdims=True)
    onehot = (lax.broadcasted_iota(jnp.int32, (classes, own), 0) == labels_ref[...]).astype(jnp.float32)
    values[1, my_gather] = (logit_scale * (probabilities - onehot)).astype(jnp.bfloat16)
    send_values(1)
    prob_ref[...] = probabilities
    new_ref[...] = coef_ref[...] - apply(1)
    for copy in sent:
        copy.wait_send()


def solution(mesh):
    rows, cols = mesh.shape["row"], mesh.shape["col"]
    cores = 2 if cols % 2 == 0 else 1
    lines, planes = cols // cores, rows * cores
    gathers, reduces = (planes, lines) if GATHER_PLANE else (lines, planes)

    def on_device(points, labels, coefficients):
        own, feat = points.shape
        classes = coefficients.shape[1]
        logit_scale = 16.0 / math.sqrt(own * rows * cols)
        vmem = pl.BlockSpec(memory_space=pltpu.VMEM)
        new, prob = pl.pallas_call(
            functools.partial(kernel, lines, planes, cores, logit_scale),
            out_shape=[jax.ShapeDtypeStruct((classes, own), jnp.float32)] * 2,
            in_specs=[vmem] * 3,
            out_specs=[vmem] * 2,
            scratch_shapes=[
                pltpu.VMEM((lines, own, 2 * feat), jnp.bfloat16),
                pltpu.VMEM((planes, own, 2 * feat), jnp.bfloat16),
                pltpu.VMEM((2, gathers, classes, own), jnp.bfloat16),
                pltpu.VMEM((gathers, own, reduces * own), jnp.bfloat16),
                pltpu.VMEM((2, reduces, classes, own), jnp.float32),
                pltpu.VMEM((2, reduces, classes, own), jnp.float32),
                pltpu.SemaphoreType.DMA((lines,)),
                pltpu.SemaphoreType.DMA((lines,)),
                pltpu.SemaphoreType.DMA((planes,)),
                pltpu.SemaphoreType.DMA((planes,)),
                pltpu.SemaphoreType.DMA((2, gathers)),
                pltpu.SemaphoreType.DMA((2, gathers)),
                pltpu.SemaphoreType.DMA((2, reduces)),
                pltpu.SemaphoreType.DMA((2, reduces)),
            ],
            compiler_params=pltpu.CompilerParams(
                collective_id=0, has_side_effects=True, vmem_limit_bytes=48 * 1024 * 1024
            ),
        )(points, labels.reshape(1, own), coefficients.T)
        return new.T, prob.T

    return jax.shard_map(
        on_device,
        mesh=mesh,
        in_specs=(P(("row", "col"), None), P(("row", "col")), P(("row", "col"), None)),
        out_specs=(P(("row", "col"), None), P(("row", "col"), None)),
        check_vma=False,
    )
```

```python
import functools
import math

import jax
import jax.numpy as jnp
from jax import lax
from jax.experimental import pallas as pl
from jax.experimental.pallas import tpu as pltpu
from jax.sharding import PartitionSpec as P

MESH = pl.DeviceIdType.MESH
NT = (((1,), (1,)), ((), ()))
NN = (((1,), (0,)), ((), ()))
GATHER_PLANE = False
LINE_ORDER = (2, 3, 1)
PLANE_ORDER = (6, 7, 2, 4, 3, 5, 1)
VALUE_ORDER = (2, 3, 1)
SUM_ORDER = (6, 7, 2, 4, 3, 5, 1)


def split_bf16(x):
    hi = x.astype(jnp.bfloat16)
    lo = (x - hi.astype(jnp.float32)).astype(jnp.bfloat16)
    return hi, lo


def peer(i, k, n):
    if n & (n - 1):
        return lax.rem(i + k, n)
    out = 0
    bit = 1
    while bit < n:
        out += ((i // bit + k // bit) % 2) * bit
        bit *= 2
    return out


def order(n, first):
    return [k for k in first if k < n] + [k for k in range(1, n) if k not in first]


def kernel(
    lines, planes, cores, logit_scale,
    points_hbm, labels_hbm, coef_hbm,
    out_ref,
    points_ref, labels_ref, coef_ref,
    line_pts, plane_pts, values, tile, partial, landed,
    line_send, line_recv, plane_send, plane_recv, value_send, value_recv, part_send, part_recv, input_sem,
):
    own, feat = points_ref.shape
    classes = coef_ref.shape[0]
    row = lax.axis_index("row")
    col = lax.axis_index("col")
    my_line = col // cores
    my_plane = row * cores + col % cores

    def line_device(i):
        return (row, i * cores + col % cores)

    def plane_device(j):
        return (j // cores, my_line * cores + j % cores)

    if GATHER_PLANE:
        gathers, my_gather, gather_device, gather_pts = planes, my_plane, plane_device, plane_pts
        reduces, my_reduce, reduce_device, reduce_pts = lines, my_line, line_device, line_pts
    else:
        gathers, my_gather, gather_device, gather_pts = lines, my_line, line_device, line_pts
        reduces, my_reduce, reduce_device, reduce_pts = planes, my_plane, plane_device, plane_pts

    loads = [
        pltpu.make_async_copy(src, dst, input_sem.at[i])
        for i, (src, dst) in enumerate(
            [(points_hbm, points_ref), (coef_hbm, coef_ref), (labels_hbm, labels_ref)]
        )
    ]
    for load in loads:
        load.start()
    barrier = pltpu.get_barrier_semaphore()
    for k in range(1, lines):
        pl.semaphore_signal(
            barrier, inc=1, device_id=line_device(peer(my_line, k, lines)), device_id_type=MESH
        )
    for k in range(1, planes):
        pl.semaphore_signal(
            barrier, inc=1, device_id=plane_device(peer(my_plane, k, planes)), device_id_type=MESH
        )

    loads[0].wait()
    hi, lo = split_bf16(points_ref[...])
    line_pts[my_line, :, :feat] = hi
    line_pts[my_line, :, feat:] = lo
    plane_pts[my_plane, :, :feat] = hi
    plane_pts[my_plane, :, feat:] = lo
    loads[1].wait()
    loads[2].wait()
    values[0, my_gather] = coef_ref[...].astype(jnp.bfloat16)
    pl.semaphore_wait(barrier, lines + planes - 2)

    def push(src, dst, send, recv, device):
        copy = pltpu.make_async_remote_copy(
            src_ref=src, dst_ref=dst, send_sem=send, recv_sem=recv, device_id=device, device_id_type=MESH
        )
        copy.start()
        return copy

    def recv_wait(buf, sem):
        pltpu.make_async_copy(buf, buf, sem).wait()

    sent = []
    for k in order(lines, LINE_ORDER):
        to = peer(my_line, k, lines)
        sent.append(push(line_pts.at[my_line], line_pts.at[my_line], line_send.at[k], line_recv.at[my_line], line_device(to)))
    for k in order(planes, PLANE_ORDER):
        to = peer(my_plane, k, planes)
        sent.append(push(plane_pts.at[my_plane], plane_pts.at[my_plane], plane_send.at[k], plane_recv.at[my_plane], plane_device(to)))

    def send_values(phase):
        for k in order(gathers, VALUE_ORDER):
            to = peer(my_gather, k, gathers)
            sent.append(push(
                values.at[phase, my_gather], values.at[phase, my_gather],
                value_send.at[phase, k], value_recv.at[phase, my_gather], gather_device(to),
            ))

    send_values(0)

    def wait_block(group, buf, recv, me, count, k):
        at = peer(me, k, count)
        recv_wait(buf.at[at], recv.at[at])
        return at

    reduce_recv = line_recv if GATHER_PLANE else plane_recv
    gather_recv = plane_recv if GATHER_PLANE else line_recv
    for k in range(1, reduces):
        wait_block("reduce", reduce_pts, reduce_recv, my_reduce, reduces, k)
    right = reduce_pts[...].reshape(reduces * own, 2 * feat)
    right_f32 = right[:, :feat].astype(jnp.float32) + right[:, feat:].astype(jnp.float32)
    sq_hi, sq_rest = split_bf16(right_f32 * right_f32)
    right_squares = lax.dot_general(
        jnp.ones((8, 2 * feat), jnp.bfloat16), jnp.concatenate([sq_hi, sq_rest], axis=1), NT,
        preferred_element_type=jnp.float32,
    )[:1]

    for k in range(gathers):
        if k == 0:
            at = my_gather
        else:
            at = wait_block("gather", gather_pts, gather_recv, my_gather, gathers, k)
        left = gather_pts[at]
        left_hi, left_lo = left[:, :feat], left[:, feat:]
        left_f32 = left_hi.astype(jnp.float32) + left_lo.astype(jnp.float32)
        left_squares = jnp.sum(left_f32 * left_f32, axis=1, keepdims=True)
        swapped = jnp.concatenate([left_lo, left_hi], axis=1)
        products = lax.dot_general(left, right, NT, preferred_element_type=jnp.float32)
        products += lax.dot_general(swapped, right, NT, preferred_element_type=jnp.float32)
        distance = left_squares + right_squares - 2.0 * products
        tile[at] = jnp.exp(distance * (-1.0 / feat)).astype(jnp.bfloat16)

    def apply(phase):
        for k in range(1, gathers):
            at = peer(my_gather, k, gathers)
            recv_wait(values.at[phase, at], value_recv.at[phase, at])
        left = jnp.concatenate([values[phase, i] for i in range(gathers)], axis=1)
        result = lax.dot_general(
            left, tile[...].reshape(gathers * own, reduces * own), NN, preferred_element_type=jnp.float32
        )
        for j in range(reduces):
            partial[phase, j] = result[:, j * own : (j + 1) * own]
        for k in order(reduces, SUM_ORDER):
            to = peer(my_reduce, k, reduces)
            sent.append(push(
                partial.at[phase, to], landed.at[phase, my_reduce],
                part_send.at[phase, k], part_recv.at[phase, my_reduce], reduce_device(to),
            ))
        total = partial[phase, my_reduce]
        for k in range(1, reduces):
            at = peer(my_reduce, k, reduces)
            recv_wait(landed.at[phase, at], part_recv.at[phase, at])
            total += landed[phase, at]
        return total

    logits = logit_scale * apply(0)
    weights = jnp.exp(logits - jnp.max(logits, axis=0, keepdims=True))
    probabilities = weights / jnp.sum(weights, axis=0, keepdims=True)
    onehot = (lax.broadcasted_iota(jnp.int32, (classes, own), 0) == labels_ref[...]).astype(jnp.float32)
    values[1, my_gather] = (logit_scale * (probabilities - onehot)).astype(jnp.bfloat16)
    send_values(1)
    out_ref[1] = -probabilities
    out_ref[0] = apply(1) - coef_ref[...]
    for copy in sent:
        copy.wait_send()


def solution(mesh):
    rows, cols = mesh.shape["row"], mesh.shape["col"]
    cores = 2 if cols % 2 == 0 else 1
    lines, planes = cols // cores, rows * cores
    gathers, reduces = (planes, lines) if GATHER_PLANE else (lines, planes)

    def on_device(points, labels, coefficients):
        own, feat = points.shape
        classes = coefficients.shape[1]
        logit_scale = 16.0 / math.sqrt(own * rows * cols)
        vmem = pl.BlockSpec(memory_space=pltpu.VMEM)
        negated = pl.pallas_call(
            functools.partial(kernel, lines, planes, cores, logit_scale),
            out_shape=jax.ShapeDtypeStruct((2, classes, own), jnp.float32),
            in_specs=[pl.BlockSpec(memory_space=pltpu.MemorySpace.HBM)] * 3,
            out_specs=vmem,
            scratch_shapes=[
                pltpu.VMEM((own, feat), jnp.float32),
                pltpu.VMEM((1, own), jnp.int32),
                pltpu.VMEM((classes, own), jnp.float32),
                pltpu.VMEM((lines, own, 2 * feat), jnp.bfloat16),
                pltpu.VMEM((planes, own, 2 * feat), jnp.bfloat16),
                pltpu.VMEM((2, gathers, classes, own), jnp.bfloat16),
                pltpu.VMEM((gathers, own, reduces * own), jnp.bfloat16),
                pltpu.VMEM((2, reduces, classes, own), jnp.float32),
                pltpu.VMEM((2, reduces, classes, own), jnp.float32),
                pltpu.SemaphoreType.DMA((lines,)),
                pltpu.SemaphoreType.DMA((lines,)),
                pltpu.SemaphoreType.DMA((planes,)),
                pltpu.SemaphoreType.DMA((planes,)),
                pltpu.SemaphoreType.DMA((2, gathers)),
                pltpu.SemaphoreType.DMA((2, gathers)),
                pltpu.SemaphoreType.DMA((2, reduces)),
                pltpu.SemaphoreType.DMA((2, reduces)),
                pltpu.SemaphoreType.DMA((3,)),
            ],
            compiler_params=pltpu.CompilerParams(
                collective_id=0, has_side_effects=True, vmem_limit_bytes=48 * 1024 * 1024
            ),
        )(*[pltpu.with_memory_space_constraint(x, pltpu.MemorySpace.HBM) for x in (points, labels.reshape(1, own), coefficients.T)])
        return -negated[0].T, -negated[1].T

    return jax.shard_map(
        on_device,
        mesh=mesh,
        in_specs=(P(("row", "col"), None), P(("row", "col")), P(("row", "col"), None)),
        out_specs=(P(("row", "col"), None), P(("row", "col"), None)),
        check_vma=False,
    )
```

```python
import functools
import math

import jax
import jax.numpy as jnp
from jax import lax
from jax.experimental import pallas as pl
from jax.experimental.pallas import tpu as pltpu
from jax.sharding import PartitionSpec as P

MESH = pl.DeviceIdType.MESH
NT = (((1,), (1,)), ((), ()))
NN = (((1,), (0,)), ((), ()))
GATHER_PLANE = False
LINE_ORDER = (2, 3, 1)
TILE_ORDER = (0, 2, 1, 3)
PLANE_ORDER = (6, 7, 2, 4, 3, 5, 1)
VALUE_ORDER = (2, 3, 1)
SUM_ORDER = (6, 7, 2, 4, 3, 5, 1)


def split_bf16(x):
    hi = x.astype(jnp.bfloat16)
    lo = (x - hi.astype(jnp.float32)).astype(jnp.bfloat16)
    return hi, lo


def peer(i, k, n):
    if n & (n - 1):
        return lax.rem(i + k, n)
    out = 0
    bit = 1
    while bit < n:
        out += ((i // bit + k // bit) % 2) * bit
        bit *= 2
    return out


def order(n, first):
    return [k for k in first if k < n] + [k for k in range(1, n) if k not in first]


def kernel(
    lines, planes, cores, logit_scale,
    points_hbm, labels_hbm, coef_hbm,
    out_ref,
    points_ref, labels_ref, coef_ref,
    line_pts, plane_pts, values, tile, partial, landed,
    line_send, line_recv, plane_send, plane_recv, value_send, value_recv, part_send, part_recv, input_sem,
):
    own, feat = points_ref.shape
    classes = coef_ref.shape[0]
    row = lax.axis_index("row")
    col = lax.axis_index("col")
    my_line = col // cores
    my_plane = row * cores + col % cores

    def line_device(i):
        return (row, i * cores + col % cores)

    def plane_device(j):
        return (j // cores, my_line * cores + j % cores)

    if GATHER_PLANE:
        gathers, my_gather, gather_device, gather_pts = planes, my_plane, plane_device, plane_pts
        reduces, my_reduce, reduce_device, reduce_pts = lines, my_line, line_device, line_pts
    else:
        gathers, my_gather, gather_device, gather_pts = lines, my_line, line_device, line_pts
        reduces, my_reduce, reduce_device, reduce_pts = planes, my_plane, plane_device, plane_pts

    loads = [
        pltpu.make_async_copy(src, dst, input_sem.at[i])
        for i, (src, dst) in enumerate(
            [(points_hbm, points_ref), (coef_hbm, coef_ref), (labels_hbm, labels_ref)]
        )
    ]
    barrier = pltpu.get_barrier_semaphore()
    for k in range(lines - 1, 0, -1):
        pl.semaphore_signal(
            barrier, inc=1, device_id=line_device(peer(my_line, k, lines)), device_id_type=MESH
        )
    for k in range(1, planes):
        pl.semaphore_signal(
            barrier, inc=1, device_id=plane_device(peer(my_plane, k, planes)), device_id_type=MESH
        )

    for load in loads:
        load.start()
    loads[0].wait()
    hi, lo = split_bf16(points_ref[...])
    line_pts[my_line, :, :feat] = hi
    line_pts[my_line, :, feat:] = lo
    plane_pts[my_plane, :, :feat] = hi
    plane_pts[my_plane, :, feat:] = lo
    loads[1].wait()
    loads[2].wait()
    values[0, my_gather] = coef_ref[...].astype(jnp.bfloat16)
    pl.semaphore_wait(barrier, lines + planes - 2)

    def push(src, dst, send, recv, device):
        copy = pltpu.make_async_remote_copy(
            src_ref=src, dst_ref=dst, send_sem=send, recv_sem=recv, device_id=device, device_id_type=MESH
        )
        copy.start()
        return copy

    def recv_wait(buf, sem):
        pltpu.make_async_copy(buf, buf, sem).wait()

    sent = []
    relay = lines == 4
    middle = (my_line == 1) | (my_line == 2)

    def line_push(src, k):
        to = peer(my_line, k, lines)
        return pltpu.make_async_remote_copy(
            src_ref=line_pts.at[src], dst_ref=line_pts.at[src],
            send_sem=line_send.at[k], recv_sem=line_recv.at[src],
            device_id=line_device(to), device_id_type=MESH,
        )

    for k in order(lines, LINE_ORDER):
        if relay and k == 3:
            @pl.when(middle)
            def _():
                line_push(my_line, 3).start()
        else:
            copy = line_push(my_line, k)
            copy.start()
            sent.append(copy)
    for k in order(planes, PLANE_ORDER):
        to = peer(my_plane, k, planes)
        sent.append(push(plane_pts.at[my_plane], plane_pts.at[my_plane], plane_send.at[k], plane_recv.at[my_plane], plane_device(to)))

    def send_values(phase):
        for k in order(gathers, VALUE_ORDER):
            to = peer(my_gather, k, gathers)
            sent.append(push(
                values.at[phase, my_gather], values.at[phase, my_gather],
                value_send.at[phase, k], value_recv.at[phase, my_gather], gather_device(to),
            ))

    send_values(0)

    def wait_block(group, buf, recv, me, count, k):
        at = peer(me, k, count)
        recv_wait(buf.at[at], recv.at[at])
        return at

    if relay:
        far = peer(my_line, 2, lines)
        recv_wait(line_pts.at[far], line_recv.at[far])

        @pl.when(middle)
        def _():
            pltpu.make_async_remote_copy(
                src_ref=line_pts.at[far], dst_ref=line_pts.at[far],
                send_sem=line_send.at[0], recv_sem=line_recv.at[far],
                device_id=line_device(peer(my_line, 1, lines)), device_id_type=MESH,
            ).start()

    reduce_recv = line_recv if GATHER_PLANE else plane_recv
    gather_recv = plane_recv if GATHER_PLANE else line_recv
    for k in range(1, reduces):
        wait_block("reduce", reduce_pts, reduce_recv, my_reduce, reduces, k)
    right = reduce_pts[...].reshape(reduces * own, 2 * feat)
    right_f32 = right[:, :feat].astype(jnp.float32) + right[:, feat:].astype(jnp.float32)
    sq_hi, sq_rest = split_bf16(right_f32 * right_f32)
    right_squares = lax.dot_general(
        jnp.ones((8, 2 * feat), jnp.bfloat16), jnp.concatenate([sq_hi, sq_rest], axis=1), NT,
        preferred_element_type=jnp.float32,
    )[:1]

    for k in TILE_ORDER if gathers == 4 else range(gathers):
        if k == 0:
            at = my_gather
        else:
            at = peer(my_gather, k, gathers)
            if not (relay and not GATHER_PLANE and k == 2):
                recv_wait(gather_pts.at[at], gather_recv.at[at])
        left = gather_pts[at]
        left_hi, left_lo = left[:, :feat], left[:, feat:]
        left_f32 = left_hi.astype(jnp.float32) + left_lo.astype(jnp.float32)
        left_squares = jnp.sum(left_f32 * left_f32, axis=1, keepdims=True)
        swapped = jnp.concatenate([left_lo, left_hi], axis=1)
        products = lax.dot_general(left, right, NT, preferred_element_type=jnp.float32)
        products += lax.dot_general(swapped, right, NT, preferred_element_type=jnp.float32)
        distance = left_squares + right_squares - 2.0 * products
        tile[at] = jnp.exp(distance * (-1.0 / feat)).astype(jnp.bfloat16)

    def apply(phase):
        for k in range(1, gathers):
            at = peer(my_gather, k, gathers)
            recv_wait(values.at[phase, at], value_recv.at[phase, at])
        left = jnp.concatenate([values[phase, i] for i in range(gathers)], axis=1)
        result = lax.dot_general(
            left, tile[...].reshape(gathers * own, reduces * own), NN, preferred_element_type=jnp.float32
        )
        for j in range(reduces):
            partial[phase, j] = result[:, j * own : (j + 1) * own]
        for k in order(reduces, SUM_ORDER):
            to = peer(my_reduce, k, reduces)
            sent.append(push(
                partial.at[phase, to], landed.at[phase, my_reduce],
                part_send.at[phase, k], part_recv.at[phase, my_reduce], reduce_device(to),
            ))
        total = partial[phase, my_reduce]
        for k in range(1, reduces):
            at = peer(my_reduce, k, reduces)
            recv_wait(landed.at[phase, at], part_recv.at[phase, at])
            total += landed[phase, at]
        return total

    logits = logit_scale * apply(0)
    weights = jnp.exp(logits - jnp.max(logits, axis=0, keepdims=True))
    probabilities = weights / jnp.sum(weights, axis=0, keepdims=True)
    onehot = (lax.broadcasted_iota(jnp.int32, (classes, own), 0) == labels_ref[...]).astype(jnp.float32)
    values[1, my_gather] = (logit_scale * (probabilities - onehot)).astype(jnp.bfloat16)
    send_values(1)
    out_ref[1] = -probabilities
    out_ref[0] = apply(1) - coef_ref[...]
    for copy in sent:
        copy.wait_send()
    if relay:
        @pl.when(middle)
        def _():
            line_push(my_line, 3).wait_send()
            pltpu.make_async_remote_copy(
                src_ref=line_pts.at[far], dst_ref=line_pts.at[far],
                send_sem=line_send.at[0], recv_sem=line_recv.at[far],
                device_id=line_device(peer(my_line, 1, lines)), device_id_type=MESH,
            ).wait_send()


def solution(mesh):
    rows, cols = mesh.shape["row"], mesh.shape["col"]
    cores = 2 if cols % 2 == 0 else 1
    lines, planes = cols // cores, rows * cores
    gathers, reduces = (planes, lines) if GATHER_PLANE else (lines, planes)

    def on_device(points, labels, coefficients):
        own, feat = points.shape
        classes = coefficients.shape[1]
        logit_scale = 16.0 / math.sqrt(own * rows * cols)
        vmem = pl.BlockSpec(memory_space=pltpu.VMEM)
        negated = pl.pallas_call(
            functools.partial(kernel, lines, planes, cores, logit_scale),
            out_shape=jax.ShapeDtypeStruct((2, classes, own), jnp.float32),
            in_specs=[pl.BlockSpec(memory_space=pltpu.MemorySpace.HBM)] * 3,
            out_specs=vmem,
            scratch_shapes=[
                pltpu.VMEM((own, feat), jnp.float32),
                pltpu.VMEM((1, own), jnp.int32),
                pltpu.VMEM((classes, own), jnp.float32),
                pltpu.VMEM((lines, own, 2 * feat), jnp.bfloat16),
                pltpu.VMEM((planes, own, 2 * feat), jnp.bfloat16),
                pltpu.VMEM((2, gathers, classes, own), jnp.bfloat16),
                pltpu.VMEM((gathers, own, reduces * own), jnp.bfloat16),
                pltpu.VMEM((2, reduces, classes, own), jnp.float32),
                pltpu.VMEM((2, reduces, classes, own), jnp.float32),
                pltpu.SemaphoreType.DMA((lines,)),
                pltpu.SemaphoreType.DMA((lines,)),
                pltpu.SemaphoreType.DMA((planes,)),
                pltpu.SemaphoreType.DMA((planes,)),
                pltpu.SemaphoreType.DMA((2, gathers)),
                pltpu.SemaphoreType.DMA((2, gathers)),
                pltpu.SemaphoreType.DMA((2, reduces)),
                pltpu.SemaphoreType.DMA((2, reduces)),
                pltpu.SemaphoreType.DMA((3,)),
            ],
            compiler_params=pltpu.CompilerParams(
                collective_id=0, has_side_effects=True, vmem_limit_bytes=48 * 1024 * 1024
            ),
        )(*[pltpu.with_memory_space_constraint(x, pltpu.MemorySpace.HBM) for x in (points, labels.reshape(1, own), coefficients.T)])
        return -negated[0].T, -negated[1].T

    return jax.shard_map(
        on_device,
        mesh=mesh,
        in_specs=(P(("row", "col"), None), P(("row", "col")), P(("row", "col"), None)),
        out_specs=(P(("row", "col"), None), P(("row", "col"), None)),
        check_vma=False,
    )
```

```python
import functools
import math

import jax
import jax.numpy as jnp
from jax import lax
from jax.experimental import pallas as pl
from jax.experimental.pallas import tpu as pltpu
from jax.sharding import PartitionSpec as P

MESH = pl.DeviceIdType.MESH
NT = (((1,), (1,)), ((), ()))
NN = (((1,), (0,)), ((), ()))
GATHER_PLANE = False
LINE_ORDER = (2, 3, 1)
TILE_ORDER = (0, 2, 1, 3)
PLANE_ORDER = (6, 7, 2, 4, 3, 5, 1)
VALUE_ORDER = (3, 2, 1)
SUM_ORDER = (6, 7, 2, 4, 3, 5, 1)


def split_bf16(x):
    hi = x.astype(jnp.bfloat16)
    lo = (x - hi.astype(jnp.float32)).astype(jnp.bfloat16)
    return hi, lo


def peer(i, k, n):
    if n & (n - 1):
        return lax.rem(i + k, n)
    out = 0
    bit = 1
    while bit < n:
        out += ((i // bit + k // bit) % 2) * bit
        bit *= 2
    return out


def order(n, first):
    return [k for k in first if k < n] + [k for k in range(1, n) if k not in first]


def kernel(
    lines, planes, cores, logit_scale,
    points_hbm, labels_hbm, coef_hbm,
    out_ref,
    points_ref, labels_ref, coef_ref,
    line_pts, plane_pts, values, tile, partial, landed,
    line_send, line_recv, plane_send, plane_recv, value_send, value_recv, part_send, part_recv, input_sem,
):
    own, feat = points_ref.shape
    classes = coef_ref.shape[0]
    row = lax.axis_index("row")
    col = lax.axis_index("col")
    my_line = col // cores
    my_plane = row * cores + col % cores

    def line_device(i):
        return (row, i * cores + col % cores)

    def plane_device(j):
        return (j // cores, my_line * cores + j % cores)

    if GATHER_PLANE:
        gathers, my_gather, gather_device, gather_pts = planes, my_plane, plane_device, plane_pts
        reduces, my_reduce, reduce_device, reduce_pts = lines, my_line, line_device, line_pts
    else:
        gathers, my_gather, gather_device, gather_pts = lines, my_line, line_device, line_pts
        reduces, my_reduce, reduce_device, reduce_pts = planes, my_plane, plane_device, plane_pts

    loads = [
        pltpu.make_async_copy(src, dst, input_sem.at[i])
        for i, (src, dst) in enumerate(
            [(points_hbm, points_ref), (coef_hbm, coef_ref), (labels_hbm, labels_ref)]
        )
    ]
    barrier = pltpu.get_barrier_semaphore()
    for k in range(lines - 1, 0, -1):
        pl.semaphore_signal(
            barrier, inc=1, device_id=line_device(peer(my_line, k, lines)), device_id_type=MESH
        )
    for k in range(1, planes):
        pl.semaphore_signal(
            barrier, inc=1, device_id=plane_device(peer(my_plane, k, planes)), device_id_type=MESH
        )

    for load in loads:
        load.start()
    loads[0].wait()
    hi, lo = split_bf16(points_ref[...])
    line_pts[my_line, :, :feat] = hi
    line_pts[my_line, :, feat:] = lo
    plane_pts[my_plane, :, :feat] = hi
    plane_pts[my_plane, :, feat:] = lo
    loads[1].wait()
    loads[2].wait()
    values[0, my_gather] = coef_ref[...].astype(jnp.bfloat16)
    pl.semaphore_wait(barrier, lines + planes - 2)

    def push(src, dst, send, recv, device):
        copy = pltpu.make_async_remote_copy(
            src_ref=src, dst_ref=dst, send_sem=send, recv_sem=recv, device_id=device, device_id_type=MESH
        )
        copy.start()
        return copy

    def recv_wait(buf, sem):
        pltpu.make_async_copy(buf, buf, sem).wait()

    sent = []
    relay = lines == 4
    middle = (my_line == 1) | (my_line == 2)

    def line_push(src, k):
        to = peer(my_line, k, lines)
        return pltpu.make_async_remote_copy(
            src_ref=line_pts.at[src], dst_ref=line_pts.at[src],
            send_sem=line_send.at[k], recv_sem=line_recv.at[src],
            device_id=line_device(to), device_id_type=MESH,
        )

    for k in order(lines, LINE_ORDER):
        if relay and k == 3:
            @pl.when(middle)
            def _():
                line_push(my_line, 3).start()
        else:
            copy = line_push(my_line, k)
            copy.start()
            sent.append(copy)
    def send_values(phase):
        for k in order(gathers, VALUE_ORDER):
            to = peer(my_gather, k, gathers)
            sent.append(push(
                values.at[phase, my_gather], values.at[phase, my_gather],
                value_send.at[phase, k], value_recv.at[phase, my_gather], gather_device(to),
            ))

    send_values(0)

    for k in order(planes, PLANE_ORDER):
        to = peer(my_plane, k, planes)
        sent.append(push(plane_pts.at[my_plane], plane_pts.at[my_plane], plane_send.at[k], plane_recv.at[my_plane], plane_device(to)))

    def wait_block(group, buf, recv, me, count, k):
        at = peer(me, k, count)
        recv_wait(buf.at[at], recv.at[at])
        return at

    if relay:
        far = peer(my_line, 2, lines)
        recv_wait(line_pts.at[far], line_recv.at[far])

        @pl.when(middle)
        def _():
            pltpu.make_async_remote_copy(
                src_ref=line_pts.at[far], dst_ref=line_pts.at[far],
                send_sem=line_send.at[0], recv_sem=line_recv.at[far],
                device_id=line_device(peer(my_line, 1, lines)), device_id_type=MESH,
            ).start()

    reduce_recv = line_recv if GATHER_PLANE else plane_recv
    gather_recv = plane_recv if GATHER_PLANE else line_recv
    for k in range(1, reduces):
        wait_block("reduce", reduce_pts, reduce_recv, my_reduce, reduces, k)
    right = reduce_pts[...].reshape(reduces * own, 2 * feat)
    right_f32 = right[:, :feat].astype(jnp.float32) + right[:, feat:].astype(jnp.float32)
    sq_hi, sq_rest = split_bf16(right_f32 * right_f32)
    right_squares = lax.dot_general(
        jnp.ones((8, 2 * feat), jnp.bfloat16), jnp.concatenate([sq_hi, sq_rest], axis=1), NT,
        preferred_element_type=jnp.float32,
    )[:1]

    for k in TILE_ORDER if gathers == 4 else range(gathers):
        if k == 0:
            at = my_gather
        else:
            at = peer(my_gather, k, gathers)
            if not (relay and not GATHER_PLANE and k == 2):
                recv_wait(gather_pts.at[at], gather_recv.at[at])
        left = gather_pts[at]
        left_hi, left_lo = left[:, :feat], left[:, feat:]
        left_f32 = left_hi.astype(jnp.float32) + left_lo.astype(jnp.float32)
        left_squares = jnp.sum(left_f32 * left_f32, axis=1, keepdims=True)
        swapped = jnp.concatenate([left_lo, left_hi], axis=1)
        products = lax.dot_general(left, right, NT, preferred_element_type=jnp.float32)
        products += lax.dot_general(swapped, right, NT, preferred_element_type=jnp.float32)
        distance = left_squares + right_squares - 2.0 * products
        tile[at] = jnp.exp(distance * (-1.0 / feat)).astype(jnp.bfloat16)

    def apply(phase):
        for k in range(1, gathers):
            at = peer(my_gather, k, gathers)
            recv_wait(values.at[phase, at], value_recv.at[phase, at])
        left = jnp.concatenate([values[phase, i] for i in range(gathers)], axis=1)
        result = lax.dot_general(
            left, tile[...].reshape(gathers * own, reduces * own), NN, preferred_element_type=jnp.float32
        )
        for j in range(reduces):
            partial[phase, j] = result[:, j * own : (j + 1) * own]
        for k in order(reduces, SUM_ORDER):
            to = peer(my_reduce, k, reduces)
            sent.append(push(
                partial.at[phase, to], landed.at[phase, my_reduce],
                part_send.at[phase, k], part_recv.at[phase, my_reduce], reduce_device(to),
            ))
        total = partial[phase, my_reduce]
        for k in range(1, reduces):
            at = peer(my_reduce, k, reduces)
            recv_wait(landed.at[phase, at], part_recv.at[phase, at])
            total += landed[phase, at]
        return total

    logits = logit_scale * apply(0)
    weights = jnp.exp(logits - jnp.max(logits, axis=0, keepdims=True))
    probabilities = weights / jnp.sum(weights, axis=0, keepdims=True)
    onehot = (lax.broadcasted_iota(jnp.int32, (classes, own), 0) == labels_ref[...]).astype(jnp.float32)
    values[1, my_gather] = (logit_scale * (probabilities - onehot)).astype(jnp.bfloat16)
    send_values(1)
    out_ref[1] = -probabilities
    out_ref[0] = apply(1) - coef_ref[...]
    for copy in sent:
        copy.wait_send()
    if relay:
        @pl.when(middle)
        def _():
            line_push(my_line, 3).wait_send()
            pltpu.make_async_remote_copy(
                src_ref=line_pts.at[far], dst_ref=line_pts.at[far],
                send_sem=line_send.at[0], recv_sem=line_recv.at[far],
                device_id=line_device(peer(my_line, 1, lines)), device_id_type=MESH,
            ).wait_send()


def solution(mesh):
    rows, cols = mesh.shape["row"], mesh.shape["col"]
    cores = 2 if cols % 2 == 0 else 1
    lines, planes = cols // cores, rows * cores
    gathers, reduces = (planes, lines) if GATHER_PLANE else (lines, planes)

    def on_device(points, labels, coefficients):
        own, feat = points.shape
        classes = coefficients.shape[1]
        logit_scale = 16.0 / math.sqrt(own * rows * cols)
        vmem = pl.BlockSpec(memory_space=pltpu.VMEM)
        negated = pl.pallas_call(
            functools.partial(kernel, lines, planes, cores, logit_scale),
            out_shape=jax.ShapeDtypeStruct((2, classes, own), jnp.float32),
            in_specs=[pl.BlockSpec(memory_space=pltpu.MemorySpace.HBM)] * 3,
            out_specs=vmem,
            scratch_shapes=[
                pltpu.VMEM((own, feat), jnp.float32),
                pltpu.VMEM((1, own), jnp.int32),
                pltpu.VMEM((classes, own), jnp.float32),
                pltpu.VMEM((lines, own, 2 * feat), jnp.bfloat16),
                pltpu.VMEM((planes, own, 2 * feat), jnp.bfloat16),
                pltpu.VMEM((2, gathers, classes, own), jnp.bfloat16),
                pltpu.VMEM((gathers, own, reduces * own), jnp.bfloat16),
                pltpu.VMEM((2, reduces, classes, own), jnp.float32),
                pltpu.VMEM((2, reduces, classes, own), jnp.float32),
                pltpu.SemaphoreType.DMA((lines,)),
                pltpu.SemaphoreType.DMA((lines,)),
                pltpu.SemaphoreType.DMA((planes,)),
                pltpu.SemaphoreType.DMA((planes,)),
                pltpu.SemaphoreType.DMA((2, gathers)),
                pltpu.SemaphoreType.DMA((2, gathers)),
                pltpu.SemaphoreType.DMA((2, reduces)),
                pltpu.SemaphoreType.DMA((2, reduces)),
                pltpu.SemaphoreType.DMA((3,)),
            ],
            compiler_params=pltpu.CompilerParams(
                collective_id=0, has_side_effects=True, vmem_limit_bytes=48 * 1024 * 1024
            ),
        )(*[pltpu.with_memory_space_constraint(x, pltpu.MemorySpace.HBM) for x in (points, labels.reshape(1, own), coefficients.T)])
        return -negated[0].T, -negated[1].T

    return jax.shard_map(
        on_device,
        mesh=mesh,
        in_specs=(P(("row", "col"), None), P(("row", "col")), P(("row", "col"), None)),
        out_specs=(P(("row", "col"), None), P(("row", "col"), None)),
        check_vma=False,
    )
```
